32 devices in a mesh: row: 16 (over z, y, x), ps: 2 (over core).
Axes of the slice: x: 2, y: 2, z: 4, core: 2. Of those that a mesh axis runs over, the one named last changes fastest.
Arguments:
- flow_state: float32 [128, 5, 16, 4, 128], P('row', None, None, 'ps'), may hold values from -1.6 to 1.6
- forcing: float32 [128, 5, 16, 4, 128], P('row', None, None, 'ps'), may hold values from -1.6 to 1.6
- harmonic_op: float32 [16, 16], replicated, may hold values from -1.5 to 1.5
- diag_inv: float32 [128, 5, 5, 4, 128], P('row', None, None, 'ps'), may hold values from -0.02 to 0.275
- lower_coupling: float32 [128, 5, 5, 4, 128], P('row', None, None, 'ps'), may hold values from -4.81 to 0.36
- upper_coupling: float32 [128, 5, 5, 4, 128], P('row', None, None, 'ps'), may hold values from -4.81 to 0.36
Outputs:
- residual: float32 [128, 5, 16, 4, 128], P('row', None, None, 'ps')
- correction: float32 [128, 5, 16, 4, 128], P('row', None, None, 'ps')
The draws below stay inside these ranges and needn't reach their ends.
All inputs are finite; a program needn't handle non-finite values.
Results may differ from the reference program's by a relative error of at most 0.00016.
Values sent between devices are 32-bit elements; how exact they have to be, the bound alone decides.
A program may use at most 192 MiB of HBM per device.

```python
import jax
import jax.numpy as jnp
from jax import lax

NC = 5
H = 16
P_SIZE = 128
NA = 128
NS = 4


def gain_draw(key):
    key_gain = jax.random.fold_in(key, 37)
    return jax.random.uniform(key_gain, (NA, 5, 1, NS, P_SIZE), jnp.float32, 0.9, 1.1)


def coupling_draw(key, salt):
    key_rate, key_noise = jax.random.split(jax.random.fold_in(key, salt))
    speed = jnp.exp(jax.random.uniform(key_rate, (NS, P_SIZE), jnp.float32, jnp.log(0.5), jnp.log(NA / 30.0)))
    decay = jnp.exp(-speed / NA)
    gains = gain_draw(key)
    noise = jnp.clip(0.02 * jax.random.normal(key_noise, (NA, 5, 5, NS, P_SIZE), jnp.float32), -0.08, 0.08)
    ident_block = jnp.eye(5, dtype=jnp.float32)[None, :, :, None, None]
    return (-(4.0 * decay[None, None, None] / gains) * (ident_block + noise)).astype(jnp.float32)


def draw_lower_coupling(key, part):
    return coupling_draw(key, 11)


def draw_upper_coupling(key, part):
    return coupling_draw(key, 23)


def draw_diag_inv(key, part):
    gains = gain_draw(key)
    key_noise = jax.random.fold_in(key, 41)
    noise = jnp.clip(0.02 * jax.random.normal(key_noise, (NA, 5, 5, NS, P_SIZE), jnp.float32), -0.08, 0.08)
    ident_block = jnp.eye(5, dtype=jnp.float32)[None, :, :, None, None]
    return (0.25 * (ident_block * gains + (1.0 - ident_block) * noise)).astype(jnp.float32)


def block_levels(rng, dims, cuts, low, largest):
    def one(position, blocks):
        steps = jax.random.uniform(jax.random.fold_in(jax.random.fold_in(rng, 6), position), (blocks,), jnp.float32, low / len(cuts), largest / len(cuts))
        return jnp.repeat(jnp.exp(steps), dims[position] // blocks).reshape((-1,) + (1,) * (len(dims) - position - 1))

    loudness = one(*cuts[0])
    for cut in cuts[1:]:
        loudness = loudness * one(*cut)
    return loudness


def gaussian(rng, dims, spread, bound, cuts=(), held_as=jnp.bfloat16):
    drawn = spread * jax.random.normal(rng, dims, jnp.float32)
    if cuts:
        drawn = drawn * block_levels(rng, dims, cuts, -0.22, 0.18)
    return jnp.clip(drawn, -bound, bound).astype(held_as)


def setup_inputs(seed: int = 0) -> dict:
    arg_keys = jax.random.split(jax.random.key(seed), 7)
    flow_state = gaussian(arg_keys[0], (NA, NC, H, NS, P_SIZE), 0.2, 1.6, ((0, 16), (3, 2)), jnp.float32)
    forcing = gaussian(arg_keys[1], (NA, NC, H, NS, P_SIZE), 0.2, 1.6, ((0, 16), (3, 2)), jnp.float32)
    harmonic_op = gaussian(arg_keys[2], (H, H), H ** -0.5, 1.5, (), jnp.float32)
    diag_inv = draw_diag_inv(jax.random.fold_in(arg_keys[6], 71), 0)
    lower_coupling = draw_lower_coupling(jax.random.fold_in(arg_keys[6], 71), 0)
    upper_coupling = draw_upper_coupling(jax.random.fold_in(arg_keys[6], 71), 0)
    return dict(flow_state=flow_state, forcing=forcing, harmonic_op=harmonic_op, diag_inv=diag_inv, lower_coupling=lower_coupling, upper_coupling=upper_coupling)


HI = lax.Precision.HIGHEST


def apply_block(block_cell, vector_cell):
    return jnp.einsum('abxp,bhxp->ahxp', block_cell, vector_cell, precision=HI)


def reference(flow_state, forcing, harmonic_op, diag_inv, lower_coupling, upper_coupling):
    padded = jnp.pad(flow_state, ((1, 1), (0, 0), (0, 0), (1, 1), (0, 0)))
    neighbours = padded[2:, :, :, 1:-1] + padded[:-2, :, :, 1:-1]
    neighbours = neighbours + padded[1:-1, :, :, 2:] + padded[1:-1, :, :, :-2]
    neighbours = neighbours + jnp.roll(flow_state, 1, 4) + jnp.roll(flow_state, -1, 4)
    coupled = jnp.einsum('gh,achsp->acgsp', harmonic_op, flow_state, precision=HI)
    residual = forcing - (1.5 * flow_state - 0.2 * neighbours + coupled)
    forward_map = -jnp.einsum('iabxp,ibcxp->iacxp', diag_inv, lower_coupling, precision=HI)
    backward_map = -jnp.einsum('iabxp,ibcxp->iacxp', diag_inv, upper_coupling, precision=HI)
    scaled = jnp.einsum('iabxp,ibhxp->iahxp', diag_inv, residual, precision=HI)
    zeros_line = jnp.zeros(residual.shape[1:], jnp.float32)

    def advance(running, inputs):
        block_cell, vector_cell = inputs
        fresh = vector_cell + apply_block(block_cell, running)
        return fresh, fresh

    _, sweep = lax.scan(advance, zeros_line, (forward_map, scaled))
    _, correction = lax.scan(advance, zeros_line, (backward_map, sweep), reverse=True)
    return residual, correction
```

```python
import functools

import jax
import jax.numpy as jnp
from jax import lax
from jax.experimental import pallas as pl
from jax.experimental.pallas import tpu as pltpu
from jax.sharding import PartitionSpec as P

MESH = pl.DeviceIdType.MESH
HI = lax.Precision.HIGHEST
NC = 5
F32 = jnp.float32
BF16 = jnp.bfloat16


def odd_rows():
    return lax.rem(lax.broadcasted_iota(jnp.int32, (8, 128), 0), 2) == 1


def spread(even, odd, mask):
    return jnp.where(mask, jnp.broadcast_to(odd, (8, 128)), jnp.broadcast_to(even, (8, 128)))


def apply(entry, columns, start=None):
    out = []
    for a in range(NC):
        total = None if start is None else start[a]
        for c in range(NC):
            term = entry(a, c)[None] * columns[c]
            total = term if total is None else total + term
        out.append(total)
    return out


def split(x):
    high = x.astype(BF16)
    return high, (x - high.astype(F32)).astype(BF16)


def kernel(n, nps, cells, flow, forcing, op, diag, lower, upper, residual, correction,
           fpad, other, force, flat, mats, maps, lead, tail, swept, corr, res, mix, work,
           summary, send_m, got_m, send_v, got_v, send_r, got_r, bounds,
           local_sem, halo_send, halo_recv, m_send, m_recv, v_send, v_recv, r_send, r_recv, out_sem):
    me, ps = lax.axis_index("row"), lax.axis_index("ps")
    per = 128 // n
    mate = 1 - ps

    loads = [
        pltpu.make_async_copy(diag, flat.at[0], local_sem.at[0]),
        pltpu.make_async_copy(lower, flat.at[1], local_sem.at[1]),
        pltpu.make_async_copy(upper, flat.at[2], local_sem.at[2]),
        pltpu.make_async_copy(flow, fpad.at[pl.ds(1, cells)], local_sem.at[3]),
        pltpu.make_async_copy(forcing, force, local_sem.at[4]),
    ]
    for load in loads:
        load.start()

    barrier = pltpu.get_barrier_semaphore()

    @pl.loop(1, n)
    def _(k):
        pl.semaphore_signal(barrier, inc=1, device_id=(lax.rem(me + k, n), ps), device_id_type=MESH)

    pl.semaphore_signal(barrier, inc=1, device_id=(me, mate), device_id_type=MESH)
    pl.semaphore_wait(barrier, n)

    to_mate = pltpu.make_async_remote_copy(
        flow, other, halo_send.at[0], halo_recv.at[0], device_id=(me, mate), device_id_type=MESH)
    up = pltpu.make_async_remote_copy(
        flow.at[cells - 1], fpad.at[0], halo_send.at[1], halo_recv.at[1],
        device_id=(lax.rem(me + 1, n), ps), device_id_type=MESH)
    down = pltpu.make_async_remote_copy(
        flow.at[0], fpad.at[cells + 1], halo_send.at[2], halo_recv.at[2],
        device_id=(lax.rem(me + n - 1, n), ps), device_id_type=MESH)
    to_mate.start()

    @pl.when(me < n - 1)
    def _():
        up.start()

    @pl.when(me > 0)
    def _():
        down.start()

    @pl.when(me == 0)
    def _():
        fpad[0] = jnp.zeros(fpad.shape[1:], F32)

    @pl.when(me == n - 1)
    def _():
        fpad[cells + 1] = jnp.zeros(fpad.shape[1:], F32)

    wide = (32, 192)
    row = lax.broadcasted_iota(jnp.int32, wide, 0)
    col = lax.broadcasted_iota(jnp.int32, wide, 1)
    part, within = col >> 5, col & 31
    left = (lax.broadcasted_iota(jnp.int32, (32, 16), 0) >> 1
            == lax.broadcasted_iota(jnp.int32, (32, 16), 1)).astype(F32)
    right = ((lax.broadcasted_iota(jnp.int32, (16, 192), 1) & 31) >> 1
             == lax.broadcasted_iota(jnp.int32, (16, 192), 0)).astype(F32)
    coupled = jnp.dot(jnp.dot(left, op[...], precision=HI, preferred_element_type=F32), right,
                      precision=HI, preferred_element_type=F32)
    swap = jnp.where((row >> 1 == within >> 1) & (row != within), F32(0.2), F32(0.0))
    coupled = jnp.where((row & 1) == (within & 1), coupled, F32(0.0))
    coef = jnp.where(part < 3, swap - coupled, jnp.where((within & 1) == ps, swap, F32(0.0)))
    rough = coef.astype(BF16).astype(F32)
    mix[...] = jnp.where((part == 2) | (part == 5), coef - rough, rough).astype(BF16)

    mask = odd_rows()
    for load in loads[:3]:
        load.wait()
    for m in range(3):
        for i in range(cells):
            mats[m, i, 0:50] = flat[m, 50 * i:50 * i + 50]
            mats[m, i, 50:56] = jnp.zeros((6, 128), F32)

    def from_diag(i):
        def entry(a, c):
            at = 10 * a + 2 * c
            return spread(mats[0, i, at:at + 1, :], mats[0, i, at + 1:at + 2, :], mask)
        return entry

    def from_maps(ref, i, base):
        def entry(a, c):
            b, at = base + (2 * c) // 8, (2 * c) % 8
            return spread(ref[i, a, b, at:at + 1, :], ref[i, a, b, at + 1:at + 2, :], mask)
        return entry

    line = lax.broadcasted_iota(jnp.int32, (2, 8, 128), 0) * 8 + lax.broadcasted_iota(jnp.int32, (2, 8, 128), 1)
    for a in range(NC):
        ident = ((line >> 1) == a).astype(F32)
        lead[0, a] = ident
        tail[cells, a, 0:2] = jnp.zeros((2, 8, 128), F32)
        tail[cells, a, 2:4] = ident

    @pl.loop(0, cells)
    def _(i):
        pairs = []
        for c in range(NC):
            low = mats[1, i, 10 * c:10 * c + 16, :].reshape(2, 8, 128)
            high = mats[2, i, 10 * c:10 * c + 16, :].reshape(2, 8, 128)
            pairs.append(jnp.concatenate([low, high], axis=0))
        made = apply(from_diag(i), pairs)
        for a in range(NC):
            maps[i, a] = -made[a]
        new = apply(from_maps(maps, i, 0), [lead[i, c] for c in range(NC)])
        for a in range(NC):
            lead[i + 1, a] = new[a]

    @pl.loop(0, cells)
    def _(k):
        i = cells - 1 - k
        start = [jnp.concatenate([lead[i + 1, a], jnp.zeros((2, 8, 128), F32)], axis=0) for a in range(NC)]
        new = apply(from_maps(maps, i, 2), [tail[i + 1, c] for c in range(NC)], start)
        for a in range(NC):
            tail[i, a] = new[a]

    def scatter_rows(value, ref):
        if per % 8 == 0:
            ref[...] = value.reshape(ref.shape)
        else:
            for j in range(n):
                ref[j, 0:per, :] = value[per * j:per * j + per, :]

    def gather_rows(ref):
        if per % 8 == 0:
            return ref[...].reshape(128, ref.shape[2])
        return jnp.concatenate([ref[j, 0:per, :] for j in range(n)], axis=0)

    def exchange(src, dst, send_sem, recv_sem):
        def copy(peer):
            return pltpu.make_async_remote_copy(
                src.at[peer], dst.at[me], send_sem.at[peer], recv_sem.at[me],
                device_id=(peer, ps), device_id_type=MESH)

        def incoming(peer):
            return pltpu.make_async_remote_copy(
                src.at[peer], dst.at[peer], send_sem.at[peer], recv_sem.at[peer],
                device_id=(peer, ps), device_id_type=MESH)

        def start():
            @pl.loop(1, n)
            def _(k):
                copy(lax.rem(me + k, n)).start()
            dst[me] = src[me]

        def wait():
            @pl.loop(1, n)
            def _(k):
                incoming(lax.rem(me + k, n)).wait_recv()

        def wait_send():
            @pl.loop(1, n)
            def _(k):
                copy(lax.rem(me + k, n)).wait_send()

        return start, wait, wait_send

    m_start, m_wait, m_sent = exchange(send_m, got_m, m_send, m_recv)
    v_start, v_wait, v_sent = exchange(send_v, got_v, v_send, v_recv)
    r_start, r_wait, r_sent = exchange(send_r, got_r, r_send, r_recv)

    for a in range(NC):
        summary[16 * a:16 * a + 16] = lead[cells, a].reshape(16, 128)
        summary[80 + 16 * a:96 + 16 * a] = tail[0, a, 0:2].reshape(16, 128)
        summary[160 + 16 * a:176 + 16 * a] = tail[0, a, 2:4].reshape(16, 128)
    summary[240:256] = jnp.zeros((16, 128), F32)
    scatter_rows(summary[0:256].T, send_m)
    m_start()

    loads[3].wait()
    loads[4].wait()
    to_mate.wait_recv()

    @pl.when(me > 0)
    def _():
        up.wait_recv()

    @pl.when(me < n - 1)
    def _():
        down.wait_recv()

    for c in range(NC):
        swept[0, c] = jnp.zeros((4, 8, 128), F32)
        corr[cells, c] = jnp.zeros((4, 8, 128), F32)

    @pl.loop(0, cells)
    def _(i):
        parts = []
        for c in range(NC):
            high, low = split(fpad[i + 1, c].reshape(32, 128))
            far_high, far_low = split(other[i, c].reshape(32, 128))
            parts.append(jnp.concatenate([high, low, high, far_high, far_low, far_high], axis=0))
        mixed = jnp.dot(mix[...], jnp.concatenate(parts, axis=1), preferred_element_type=F32)
        rows = []
        for c in range(NC):
            mine = fpad[i + 1, c]
            flatm = mine.reshape(32, 128)
            around = (fpad[i, c] + fpad[i + 2, c]
                      + (pltpu.roll(flatm, 1, 1) + pltpu.roll(flatm, 127, 1)).reshape(4, 8, 128))
            r = (force[i, c] - 1.5 * mine + 0.2 * around
                 + mixed[:, 128 * c:128 * c + 128].reshape(4, 8, 128))
            res[i, c] = r
            rows.append(r)
        scaled = apply(from_diag(i), rows)
        new = apply(from_maps(maps, i, 0), [swept[i, c] for c in range(NC)], scaled)
        for a in range(NC):
            swept[i + 1, a] = new[a]

    out_res = pltpu.make_async_copy(res, residual, out_sem.at[0])
    out_res.start()

    @pl.loop(0, cells)
    def _(k):
        i = cells - 1 - k
        new = apply(from_maps(maps, i, 2), [corr[i + 1, c] for c in range(NC)],
                    [swept[i + 1, a] for a in range(NC)])
        for a in range(NC):
            corr[i, a] = new[a]

    for a in range(NC):
        summary[32 * a:32 * a + 32] = swept[cells, a].reshape(32, 128)
        summary[160 + 32 * a:192 + 32 * a] = corr[0, a].reshape(32, 128)
    summary[320:384] = jnp.zeros((64, 128), F32)
    scatter_rows(summary[...].T, send_v)
    v_start()
    m_wait()
    bounds[0:256] = gather_rows(got_m).T
    v_wait()
    summary[...] = gather_rows(got_v).T
    lane = lax.broadcasted_iota(jnp.int32, (8, 128), 1)[None]
    steps = n.bit_length() - 1

    def shift(x, by):
        blocks = x.shape[0]
        return pltpu.roll(x.reshape(8 * blocks, 128), by, 1).reshape(blocks, 8, 128)

    for a in range(NC):
        work[0, a, 0:4] = summary[32 * a:32 * a + 32].reshape(4, 8, 128)
        work[0, a, 4:6] = bounds[16 * a:16 * a + 16].reshape(2, 8, 128)
        work[1, a, 4:6] = bounds[160 + 16 * a:176 + 16 * a].reshape(2, 8, 128)

    def scan(which, backward):
        @pl.loop(0, steps)
        def _(k):
            by = jnp.left_shift(per, k)
            turn = 128 - by if backward else by
            inside = lane < 128 - by if backward else lane >= by
            moved = [shift(work[which, c], turn) for c in range(NC)]
            old = [work[which, a] for a in range(NC)]
            start = [jnp.concatenate([old[a][0:4], jnp.zeros((2, 8, 128), F32)], axis=0) for a in range(NC)]
            new = apply(from_maps(work, which, 4), moved, start)
            for a in range(NC):
                work[which, a] = jnp.where(inside, new[a], old[a])

    scan(0, False)
    entering = [jnp.where(lane >= per, shift(work[0, a, 0:4], per), F32(0.0)) for a in range(NC)]

    def from_tail(a, c):
        at = 80 + 16 * a + 2 * c
        return spread(bounds[at:at + 1, :], bounds[at + 1:at + 2, :], mask)

    last = apply(from_tail, entering, [summary[160 + 32 * a:192 + 32 * a].reshape(4, 8, 128) for a in range(NC)])
    for a in range(NC):
        work[1, a, 0:4] = last[a]
        summary[32 * a:32 * a + 32] = entering[a].reshape(32, 128)
    scan(1, True)
    for a in range(NC):
        back = jnp.where(lane < 128 - per, shift(work[1, a, 0:4], 128 - per), F32(0.0))
        summary[160 + 32 * a:192 + 32 * a] = back.reshape(32, 128)
    scatter_rows(summary[...].T, send_r)
    r_start()
    r_wait()
    bounds[...] = gather_rows(got_r).T

    @pl.loop(0, cells)
    def _(i):
        first = [bounds[32 * c:32 * c + 32].reshape(4, 8, 128) for c in range(NC)]
        new = apply(from_maps(tail, i, 0), first, [corr[i, a] for a in range(NC)])
        second = [bounds[160 + 32 * c:192 + 32 * c].reshape(4, 8, 128) for c in range(NC)]
        new = apply(from_maps(tail, i, 2), second, new)
        for a in range(NC):
            corr[i, a] = new[a]

    out_corr = pltpu.make_async_copy(corr.at[pl.ds(0, cells)], correction, out_sem.at[1])
    out_corr.start()
    to_mate.wait_send()

    @pl.when(me < n - 1)
    def _():
        up.wait_send()

    @pl.when(me > 0)
    def _():
        down.wait_send()

    m_sent()
    v_sent()
    r_sent()
    out_res.wait()
    out_corr.wait()


def body(n, nps, flow, forcing, op, diag, lower, upper):
    cells = flow.shape[0]
    whole = flow.shape
    state = (cells, NC, 4, 8, 128)
    rows = max(8, 128 // n)
    vmem, dma = pltpu.VMEM, pltpu.SemaphoreType.DMA
    spec_any = pl.BlockSpec(memory_space=pl.ANY)
    spec_vmem = pl.BlockSpec(memory_space=pltpu.VMEM)
    residual, correction = pl.pallas_call(
        functools.partial(kernel, n, nps, cells),
        out_shape=[jax.ShapeDtypeStruct(state, F32)] * 2,
        in_specs=[spec_any, spec_any, spec_vmem, spec_any, spec_any, spec_any],
        out_specs=[spec_any, spec_any],
        scratch_shapes=[
            vmem((cells + 2,) + state[1:], F32),
            vmem(state, F32),
            vmem(state, F32),
            vmem((3, 50 * cells, 128), F32),
            vmem((3, cells, 56, 128), F32),
            vmem(state, F32),
            vmem((cells + 1, NC, 2, 8, 128), F32),
            vmem((cells + 1,) + state[1:], F32),
            vmem((cells + 1,) + state[1:], F32),
            vmem((cells + 1,) + state[1:], F32),
            vmem(state, F32),
            vmem((32, 192), BF16),
            vmem((2, NC, 6, 8, 128), F32),
            vmem((384, 128), F32),
            vmem((n, rows, 256), F32),
            vmem((n, rows, 256), F32),
            vmem((n, rows, 384), F32),
            vmem((n, rows, 384), F32),
            vmem((n, rows, 384), F32),
            vmem((n, rows, 384), F32),
            vmem((384, 128), F32),
            dma((5,)), dma((3,)), dma((3,)),
            dma((n,)), dma((n,)), dma((n,)), dma((n,)), dma((n,)), dma((n,)),
            dma((2,)),
        ],
        compiler_params=pltpu.CompilerParams(
            collective_id=0, has_side_effects=True, vmem_limit_bytes=40 * 1024 * 1024),
    )(flow.reshape(state), forcing.reshape(state), op,
      diag.reshape(50 * cells, 128), lower.reshape(50 * cells, 128), upper.reshape(50 * cells, 128))
    return residual.reshape(whole), correction.reshape(whole)


def solution(mesh):
    spec = P("row", None, None, "ps", None)
    return jax.shard_map(
        functools.partial(body, mesh.shape["row"], mesh.shape["ps"]),
        mesh=mesh,
        in_specs=(spec, spec, P(), spec, spec, spec),
        out_specs=(spec, spec),
        check_vma=False,
    )
```

```python
import functools

import jax
import jax.numpy as jnp
from jax import lax
from jax.experimental import pallas as pl
from jax.experimental.pallas import tpu as pltpu
from jax.sharding import PartitionSpec as P

MESH = pl.DeviceIdType.MESH
HI = lax.Precision.HIGHEST
NC = 5
F32 = jnp.float32
BF16 = jnp.bfloat16


def odd_rows():
    return lax.rem(lax.broadcasted_iota(jnp.int32, (8, 128), 0), 2) == 1


def spread(even, odd, mask):
    return jnp.where(mask, jnp.broadcast_to(odd, (8, 128)), jnp.broadcast_to(even, (8, 128)))


def apply(entry, columns, start=None):
    out = []
    for a in range(NC):
        total = None if start is None else start[a]
        for c in range(NC):
            term = entry(a, c)[None] * columns[c]
            total = term if total is None else total + term
        out.append(total)
    return out


def split(x):
    high = x.astype(BF16)
    return high, (x - high.astype(F32)).astype(BF16)


def kernel(n, nps, cells, flow, forcing, op, diag, lower, upper, residual, correction,
           fpad, other, below, above, force, flat, mats, maps, lead, tail, swept, corr, res, mix, work,
           summary, send_m, got_m, send_v, got_v, send_r, got_r, bounds,
           local_sem, halo_send, halo_recv, m_send, m_recv, v_send, v_recv, r_send, r_recv, out_sem):
    me, ps = lax.axis_index("row"), lax.axis_index("ps")
    per = 128 // n
    mate = 1 - ps

    loads = [
        pltpu.make_async_copy(diag, flat.at[0], local_sem.at[0]),
        pltpu.make_async_copy(lower, flat.at[1], local_sem.at[1]),
        pltpu.make_async_copy(upper, flat.at[2], local_sem.at[2]),
        pltpu.make_async_copy(flow, fpad.at[pl.ds(1, cells)], local_sem.at[3]),
        pltpu.make_async_copy(forcing, force, local_sem.at[4]),
    ]
    for load in loads:
        load.start()

    barrier = pltpu.get_barrier_semaphore()

    @pl.loop(1, n)
    def _(k):
        pl.semaphore_signal(barrier, inc=1, device_id=(lax.rem(me + k, n), ps), device_id_type=MESH)

    pl.semaphore_signal(barrier, inc=1, device_id=(me, mate), device_id_type=MESH)

    wide = (32, 192)
    row = lax.broadcasted_iota(jnp.int32, wide, 0)
    col = lax.broadcasted_iota(jnp.int32, wide, 1)
    part, within = col >> 5, col & 31
    left = (lax.broadcasted_iota(jnp.int32, (32, 16), 0) >> 1
            == lax.broadcasted_iota(jnp.int32, (32, 16), 1)).astype(F32)
    right = ((lax.broadcasted_iota(jnp.int32, (16, 192), 1) & 31) >> 1
             == lax.broadcasted_iota(jnp.int32, (16, 192), 0)).astype(F32)
    coupled = jnp.dot(jnp.dot(left, op[...], precision=HI, preferred_element_type=F32), right,
                      precision=HI, preferred_element_type=F32)
    swap = jnp.where((row >> 1 == within >> 1) & (row != within), F32(0.2), F32(0.0))
    coupled = jnp.where((row & 1) == (within & 1), coupled, F32(0.0))
    coef = jnp.where(part < 3, swap - coupled, jnp.where((within & 1) == ps, swap, F32(0.0)))
    rough = coef.astype(BF16).astype(F32)
    pieces = jnp.where((part == 2) | (part == 5), coef - rough, rough).astype(BF16)
    mix[0] = pieces[:, 0:96]
    mix[1] = pieces[:, 96:192]

    mask = odd_rows()
    for load in loads[:3]:
        load.wait()
    for m in range(3):
        for i in range(cells):
            mats[m, i, 0:50] = flat[m, 50 * i:50 * i + 50]
            mats[m, i, 50:56] = jnp.zeros((6, 128), F32)

    def from_diag(i):
        def entry(a, c):
            at = 10 * a + 2 * c
            return spread(mats[0, i, at:at + 1, :], mats[0, i, at + 1:at + 2, :], mask)
        return entry

    def from_maps(ref, i, base):
        def entry(a, c):
            b, at = base + (2 * c) // 8, (2 * c) % 8
            return spread(ref[i, a, b, at:at + 1, :], ref[i, a, b, at + 1:at + 2, :], mask)
        return entry

    line = lax.broadcasted_iota(jnp.int32, (2, 8, 128), 0) * 8 + lax.broadcasted_iota(jnp.int32, (2, 8, 128), 1)
    for a in range(NC):
        ident = ((line >> 1) == a).astype(F32)
        lead[0, a] = ident
        tail[cells, a, 0:2] = jnp.zeros((2, 8, 128), F32)
        tail[cells, a, 2:4] = ident

    @pl.loop(0, cells)
    def _(i):
        pairs = []
        for c in range(NC):
            low = mats[1, i, 10 * c:10 * c + 16, :].reshape(2, 8, 128)
            high = mats[2, i, 10 * c:10 * c + 16, :].reshape(2, 8, 128)
            pairs.append(jnp.concatenate([low, high], axis=0))
        made = apply(from_diag(i), pairs)
        for a in range(NC):
            maps[i, a] = -made[a]
        new = apply(from_maps(maps, i, 0), [lead[i, c] for c in range(NC)])
        for a in range(NC):
            lead[i + 1, a] = new[a]

    @pl.loop(0, cells)
    def _(k):
        i = cells - 1 - k
        start = [jnp.concatenate([lead[i + 1, a], jnp.zeros((2, 8, 128), F32)], axis=0) for a in range(NC)]
        new = apply(from_maps(maps, i, 2), [tail[i + 1, c] for c in range(NC)], start)
        for a in range(NC):
            tail[i, a] = new[a]

    def scatter_rows(value, ref):
        if per % 8 == 0:
            ref[...] = value.reshape(ref.shape)
        else:
            for j in range(n):
                ref[j, 0:per, :] = value[per * j:per * j + per, :]

    def gather_rows(ref):
        if per % 8 == 0:
            return ref[...].reshape(128, ref.shape[2])
        return jnp.concatenate([ref[j, 0:per, :] for j in range(n)], axis=0)

    def exchange(src, dst, send_sem, recv_sem):
        def copy(peer):
            return pltpu.make_async_remote_copy(
                src.at[peer], dst.at[me], send_sem.at[peer], recv_sem.at[me],
                device_id=(peer, ps), device_id_type=MESH)

        def incoming(peer):
            return pltpu.make_async_remote_copy(
                src.at[peer], dst.at[peer], send_sem.at[peer], recv_sem.at[peer],
                device_id=(peer, ps), device_id_type=MESH)

        def start():
            @pl.loop(1, n)
            def _(k):
                copy(lax.rem(me + k, n)).start()
            dst[me] = src[me]

        def wait():
            @pl.loop(1, n)
            def _(k):
                incoming(lax.rem(me + k, n)).wait_recv()

        def wait_send():
            @pl.loop(1, n)
            def _(k):
                copy(lax.rem(me + k, n)).wait_send()

        return start, wait, wait_send

    m_start, m_wait, m_sent = exchange(send_m, got_m, m_send, m_recv)
    v_start, v_wait, v_sent = exchange(send_v, got_v, v_send, v_recv)
    r_start, r_wait, r_sent = exchange(send_r, got_r, r_send, r_recv)

    for a in range(NC):
        summary[16 * a:16 * a + 16] = lead[cells, a].reshape(16, 128)
        summary[80 + 16 * a:96 + 16 * a] = tail[0, a, 0:2].reshape(16, 128)
        summary[160 + 16 * a:176 + 16 * a] = tail[0, a, 2:4].reshape(16, 128)
    summary[240:256] = jnp.zeros((16, 128), F32)
    scatter_rows(summary[0:256].T, send_m)
    loads[3].wait()
    loads[4].wait()
    fpad[0] = jnp.zeros(fpad.shape[1:], F32)
    fpad[cells + 1] = jnp.zeros(fpad.shape[1:], F32)

    def mixed(ref, i, first):
        parts = []
        for c in range(NC):
            high, low = split(ref[i, c].reshape(32, 128))
            parts.append(jnp.concatenate([high, low, high], axis=0))
        return jnp.dot(mix[first], jnp.concatenate(parts, axis=1), preferred_element_type=F32)

    @pl.loop(0, cells)
    def _(i):
        sums = mixed(fpad, i + 1, 0)
        for c in range(NC):
            mine = fpad[i + 1, c]
            flatm = mine.reshape(32, 128)
            around = (fpad[i, c] + fpad[i + 2, c]
                      + (pltpu.roll(flatm, 1, 1) + pltpu.roll(flatm, 127, 1)).reshape(4, 8, 128))
            res[i, c] = (force[i, c] - 1.5 * mine + 0.2 * around
                         + sums[:, 128 * c:128 * c + 128].reshape(4, 8, 128))

    pl.semaphore_wait(barrier, n)
    to_mate = pltpu.make_async_remote_copy(
        fpad.at[pl.ds(1, cells)], other, halo_send.at[0], halo_recv.at[0], device_id=(me, mate), device_id_type=MESH)
    up = pltpu.make_async_remote_copy(
        fpad.at[cells], below, halo_send.at[1], halo_recv.at[1],
        device_id=(lax.rem(me + 1, n), ps), device_id_type=MESH)
    down = pltpu.make_async_remote_copy(
        fpad.at[1], above, halo_send.at[2], halo_recv.at[2],
        device_id=(lax.rem(me + n - 1, n), ps), device_id_type=MESH)
    to_mate.start()

    @pl.when(me < n - 1)
    def _():
        up.start()

    @pl.when(me > 0)
    def _():
        down.start()

    m_start()
    to_mate.wait_recv()

    @pl.when(me > 0)
    def _():
        up.wait_recv()
        res[0] += 0.2 * below[...]

    @pl.when(me < n - 1)
    def _():
        down.wait_recv()
        res[cells - 1] += 0.2 * above[...]

    for c in range(NC):
        swept[0, c] = jnp.zeros((4, 8, 128), F32)
        corr[cells, c] = jnp.zeros((4, 8, 128), F32)

    @pl.loop(0, cells)
    def _(i):
        sums = mixed(other, i, 1)
        rows = []
        for c in range(NC):
            r = res[i, c] + sums[:, 128 * c:128 * c + 128].reshape(4, 8, 128)
            res[i, c] = r
            rows.append(r)
        scaled = apply(from_diag(i), rows)
        new = apply(from_maps(maps, i, 0), [swept[i, c] for c in range(NC)], scaled)
        for a in range(NC):
            swept[i + 1, a] = new[a]

    out_res = pltpu.make_async_copy(res, residual, out_sem.at[0])
    out_res.start()

    @pl.loop(0, cells)
    def _(k):
        i = cells - 1 - k
        new = apply(from_maps(maps, i, 2), [corr[i + 1, c] for c in range(NC)],
                    [swept[i + 1, a] for a in range(NC)])
        for a in range(NC):
            corr[i, a] = new[a]

    for a in range(NC):
        summary[32 * a:32 * a + 32] = swept[cells, a].reshape(32, 128)
        summary[160 + 32 * a:192 + 32 * a] = corr[0, a].reshape(32, 128)
    summary[320:384] = jnp.zeros((64, 128), F32)
    scatter_rows(summary[...].T, send_v)
    v_start()
    m_wait()
    bounds[0:256] = gather_rows(got_m).T
    v_wait()
    summary[...] = gather_rows(got_v).T
    lane = lax.broadcasted_iota(jnp.int32, (8, 128), 1)[None]
    steps = n.bit_length() - 1

    def shift(x, by):
        blocks = x.shape[0]
        return pltpu.roll(x.reshape(8 * blocks, 128), by, 1).reshape(blocks, 8, 128)

    for a in range(NC):
        work[0, a, 0:4] = summary[32 * a:32 * a + 32].reshape(4, 8, 128)
        work[0, a, 4:6] = bounds[16 * a:16 * a + 16].reshape(2, 8, 128)
        work[1, a, 4:6] = bounds[160 + 16 * a:176 + 16 * a].reshape(2, 8, 128)

    def scan(which, backward):
        @pl.loop(0, steps)
        def _(k):
            by = jnp.left_shift(per, k)
            turn = 128 - by if backward else by
            inside = lane < 128 - by if backward else lane >= by
            moved = [shift(work[which, c], turn) for c in range(NC)]
            old = [work[which, a] for a in range(NC)]
            start = [jnp.concatenate([old[a][0:4], jnp.zeros((2, 8, 128), F32)], axis=0) for a in range(NC)]
            new = apply(from_maps(work, which, 4), moved, start)
            for a in range(NC):
                work[which, a] = jnp.where(inside, new[a], old[a])

    scan(0, False)
    entering = [jnp.where(lane >= per, shift(work[0, a, 0:4], per), F32(0.0)) for a in range(NC)]

    def from_tail(a, c):
        at = 80 + 16 * a + 2 * c
        return spread(bounds[at:at + 1, :], bounds[at + 1:at + 2, :], mask)

    last = apply(from_tail, entering, [summary[160 + 32 * a:192 + 32 * a].reshape(4, 8, 128) for a in range(NC)])
    for a in range(NC):
        work[1, a, 0:4] = last[a]
        summary[32 * a:32 * a + 32] = entering[a].reshape(32, 128)
    scan(1, True)
    for a in range(NC):
        back = jnp.where(lane < 128 - per, shift(work[1, a, 0:4], 128 - per), F32(0.0))
        summary[160 + 32 * a:192 + 32 * a] = back.reshape(32, 128)
    scatter_rows(summary[...].T, send_r)
    r_start()
    r_wait()
    bounds[...] = gather_rows(got_r).T

    @pl.loop(0, cells)
    def _(i):
        first = [bounds[32 * c:32 * c + 32].reshape(4, 8, 128) for c in range(NC)]
        new = apply(from_maps(tail, i, 0), first, [corr[i, a] for a in range(NC)])
        second = [bounds[160 + 32 * c:192 + 32 * c].reshape(4, 8, 128) for c in range(NC)]
        new = apply(from_maps(tail, i, 2), second, new)
        for a in range(NC):
            corr[i, a] = new[a]

    out_corr = pltpu.make_async_copy(corr.at[pl.ds(0, cells)], correction, out_sem.at[1])
    out_corr.start()
    to_mate.wait_send()

    @pl.when(me < n - 1)
    def _():
        up.wait_send()

    @pl.when(me > 0)
    def _():
        down.wait_send()

    m_sent()
    v_sent()
    r_sent()
    out_res.wait()
    out_corr.wait()


def body(n, nps, flow, forcing, op, diag, lower, upper):
    cells = flow.shape[0]
    whole = flow.shape
    state = (cells, NC, 4, 8, 128)
    rows = max(8, 128 // n)
    vmem, dma = pltpu.VMEM, pltpu.SemaphoreType.DMA
    spec_any = pl.BlockSpec(memory_space=pltpu.HBM)
    spec_vmem = pl.BlockSpec(memory_space=pltpu.VMEM)
    residual, correction = pl.pallas_call(
        functools.partial(kernel, n, nps, cells),
        out_shape=[jax.ShapeDtypeStruct(state, F32)] * 2,
        in_specs=[spec_any, spec_any, spec_vmem, spec_any, spec_any, spec_any],
        out_specs=[spec_any, spec_any],
        scratch_shapes=[
            vmem((cells + 2,) + state[1:], F32),
            vmem(state, F32),
            vmem(state[1:], F32),
            vmem(state[1:], F32),
            vmem(state, F32),
            vmem((3, 50 * cells, 128), F32),
            vmem((3, cells, 56, 128), F32),
            vmem(state, F32),
            vmem((cells + 1, NC, 2, 8, 128), F32),
            vmem((cells + 1,) + state[1:], F32),
            vmem((cells + 1,) + state[1:], F32),
            vmem((cells + 1,) + state[1:], F32),
            vmem(state, F32),
            vmem((2, 32, 96), BF16),
            vmem((2, NC, 6, 8, 128), F32),
            vmem((384, 128), F32),
            vmem((n, rows, 256), F32),
            vmem((n, rows, 256), F32),
            vmem((n, rows, 384), F32),
            vmem((n, rows, 384), F32),
            vmem((n, rows, 384), F32),
            vmem((n, rows, 384), F32),
            vmem((384, 128), F32),
            dma((5,)), dma((3,)), dma((3,)),
            dma((n,)), dma((n,)), dma((n,)), dma((n,)), dma((n,)), dma((n,)),
            dma((2,)),
        ],
        compiler_params=pltpu.CompilerParams(
            collective_id=0, has_side_effects=True, vmem_limit_bytes=60 * 1024 * 1024),
    )(flow.reshape(state), forcing.reshape(state), op,
      diag.reshape(50 * cells, 128), lower.reshape(50 * cells, 128), upper.reshape(50 * cells, 128))
    return residual.reshape(whole), correction.reshape(whole)


def solution(mesh):
    spec = P("row", None, None, "ps", None)
    return jax.shard_map(
        functools.partial(body, mesh.shape["row"], mesh.shape["ps"]),
        mesh=mesh,
        in_specs=(spec, spec, P(), spec, spec, spec),
        out_specs=(spec, spec),
        check_vma=False,
    )
```

```python
import functools

import jax
import jax.numpy as jnp
from jax import lax
from jax.experimental import pallas as pl
from jax.experimental.pallas import tpu as pltpu
from jax.sharding import PartitionSpec as P

MESH = pl.DeviceIdType.MESH
HI = lax.Precision.HIGHEST
NC = 5
F32 = jnp.float32
BF16 = jnp.bfloat16


def odd_rows():
    return lax.rem(lax.broadcasted_iota(jnp.int32, (8, 128), 0), 2) == 1


def spread(even, odd, mask):
    return jnp.where(mask, jnp.broadcast_to(odd, (8, 128)), jnp.broadcast_to(even, (8, 128)))


def apply(entry, columns, start=None):
    out = []
    for a in range(NC):
        total = None if start is None else start[a]
        for c in range(NC):
            term = entry(a, c)[None] * columns[c]
            total = term if total is None else total + term
        out.append(total)
    return out


def split(x):
    high = x.astype(BF16)
    return high, (x - high.astype(F32)).astype(BF16)


def kernel(n, nps, cells, flow, forcing, op, diag, lower, upper, res, correction,
           harmonics, fpad, other, below, above, force, flat, mats, maps, lead, tail, swept, corr, mix, work,
           summary, send_m, got_m, send_v, got_v, send_r, got_r, bounds,
           local_sem, halo_send, halo_recv, m_send, m_recv, v_send, v_recv, r_send, r_recv):
    me, ps = lax.axis_index("row"), lax.axis_index("ps")
    per = 128 // n
    mate = 1 - ps

    loads = [
        pltpu.make_async_copy(diag, flat.at[0], local_sem.at[0]),
        pltpu.make_async_copy(lower, flat.at[1], local_sem.at[1]),
        pltpu.make_async_copy(upper, flat.at[2], local_sem.at[2]),
        pltpu.make_async_copy(flow, fpad.at[pl.ds(1, cells)], local_sem.at[3]),
        pltpu.make_async_copy(forcing, force, local_sem.at[4]),
        pltpu.make_async_copy(op, harmonics, local_sem.at[5]),
    ]
    for load in loads:
        load.start()

    barrier = pltpu.get_barrier_semaphore()

    @pl.loop(1, n)
    def _(k):
        pl.semaphore_signal(barrier, inc=1, device_id=(lax.rem(me + k, n), ps), device_id_type=MESH)

    pl.semaphore_signal(barrier, inc=1, device_id=(me, mate), device_id_type=MESH)

    pl.semaphore_wait(barrier, n)
    to_mate = pltpu.make_async_remote_copy(
        flow, other, halo_send.at[0], halo_recv.at[0], device_id=(me, mate), device_id_type=MESH)
    up = pltpu.make_async_remote_copy(
        flow.at[cells - 1], below, halo_send.at[1], halo_recv.at[1],
        device_id=(lax.rem(me + 1, n), ps), device_id_type=MESH)
    down = pltpu.make_async_remote_copy(
        flow.at[0], above, halo_send.at[2], halo_recv.at[2],
        device_id=(lax.rem(me + n - 1, n), ps), device_id_type=MESH)
    to_mate.start()

    @pl.when(me < n - 1)
    def _():
        up.start()

    @pl.when(me > 0)
    def _():
        down.start()

    wide = (32, 192)
    row = lax.broadcasted_iota(jnp.int32, wide, 0)
    col = lax.broadcasted_iota(jnp.int32, wide, 1)
    part, within = col >> 5, col & 31
    left = (lax.broadcasted_iota(jnp.int32, (32, 16), 0) >> 1
            == lax.broadcasted_iota(jnp.int32, (32, 16), 1)).astype(F32)
    right = ((lax.broadcasted_iota(jnp.int32, (16, 192), 1) & 31) >> 1
             == lax.broadcasted_iota(jnp.int32, (16, 192), 0)).astype(F32)
    loads[5].wait()
    coupled = jnp.dot(jnp.dot(left, harmonics[...], precision=HI, preferred_element_type=F32), right,
                      precision=HI, preferred_element_type=F32)
    swap = jnp.where((row >> 1 == within >> 1) & (row != within), F32(0.2), F32(0.0))
    coupled = jnp.where((row & 1) == (within & 1), coupled, F32(0.0))
    coef = jnp.where(part < 3, swap - coupled, jnp.where((within & 1) == ps, swap, F32(0.0)))
    rough = coef.astype(BF16).astype(F32)
    pieces = jnp.where((part == 2) | (part == 5), coef - rough, rough).astype(BF16)
    mix[0] = pieces[:, 0:96]
    mix[1] = pieces[:, 96:192]

    mask = odd_rows()
    for load in loads[:3]:
        load.wait()
    for m in range(3):
        for i in range(cells):
            mats[m, i, 0:50] = flat[m, 50 * i:50 * i + 50]
            mats[m, i, 50:56] = jnp.zeros((6, 128), F32)

    def from_diag(i):
        def entry(a, c):
            at = 10 * a + 2 * c
            return spread(mats[0, i, at:at + 1, :], mats[0, i, at + 1:at + 2, :], mask)
        return entry

    def from_maps(ref, i, base):
        def entry(a, c):
            b, at = base + (2 * c) // 8, (2 * c) % 8
            return spread(ref[i, a, b, at:at + 1, :], ref[i, a, b, at + 1:at + 2, :], mask)
        return entry

    line = lax.broadcasted_iota(jnp.int32, (2, 8, 128), 0) * 8 + lax.broadcasted_iota(jnp.int32, (2, 8, 128), 1)
    for a in range(NC):
        ident = ((line >> 1) == a).astype(F32)
        lead[0, a] = ident
        tail[cells, a, 0:2] = jnp.zeros((2, 8, 128), F32)
        tail[cells, a, 2:4] = ident

    @pl.loop(0, cells)
    def _(i):
        pairs = []
        for c in range(NC):
            low = mats[1, i, 10 * c:10 * c + 16, :].reshape(2, 8, 128)
            high = mats[2, i, 10 * c:10 * c + 16, :].reshape(2, 8, 128)
            pairs.append(jnp.concatenate([low, high], axis=0))
        made = apply(from_diag(i), pairs)
        for a in range(NC):
            maps[i, a] = -made[a]
        new = apply(from_maps(maps, i, 0), [lead[i, c] for c in range(NC)])
        for a in range(NC):
            lead[i + 1, a] = new[a]

    @pl.loop(0, cells)
    def _(k):
        i = cells - 1 - k
        start = [jnp.concatenate([lead[i + 1, a], jnp.zeros((2, 8, 128), F32)], axis=0) for a in range(NC)]
        new = apply(from_maps(maps, i, 2), [tail[i + 1, c] for c in range(NC)], start)
        for a in range(NC):
            tail[i, a] = new[a]

    def scatter_rows(value, ref):
        if per % 8 == 0:
            ref[...] = value.reshape(ref.shape)
        else:
            for j in range(n):
                ref[j, 0:per, :] = value[per * j:per * j + per, :]

    def gather_rows(ref):
        if per % 8 == 0:
            return ref[...].reshape(128, ref.shape[2])
        return jnp.concatenate([ref[j, 0:per, :] for j in range(n)], axis=0)

    def exchange(src, dst, send_sem, recv_sem):
        def start():
            for k in range(1, n):
                peer = lax.rem(me + k, n)
                pltpu.make_async_remote_copy(
                    src.at[peer], dst.at[me], send_sem, recv_sem,
                    device_id=(peer, ps), device_id_type=MESH).start()
            dst[me] = src[me]

        every = pltpu.make_async_remote_copy(
            src.at[pl.ds(0, n - 1)], dst.at[pl.ds(0, n - 1)], send_sem, recv_sem,
            device_id=(lax.rem(me + 1, n), ps), device_id_type=MESH)
        return start, every.wait_recv, every.wait_send

    m_start, m_wait, m_sent = exchange(send_m, got_m, m_send.at[0], m_recv.at[0])
    v_start, v_wait, v_sent = exchange(send_v, got_v, v_send.at[0], v_recv.at[0])
    r_start, r_wait, r_sent = exchange(send_r, got_r, r_send.at[0], r_recv.at[0])

    for a in range(NC):
        summary[16 * a:16 * a + 16] = lead[cells, a].reshape(16, 128)
        summary[80 + 16 * a:96 + 16 * a] = tail[0, a, 0:2].reshape(16, 128)
        summary[160 + 16 * a:176 + 16 * a] = tail[0, a, 2:4].reshape(16, 128)
    summary[240:256] = jnp.zeros((16, 128), F32)
    scatter_rows(summary[0:256].T, send_m)
    m_start()
    loads[3].wait()
    loads[4].wait()
    fpad[0] = jnp.zeros(fpad.shape[1:], F32)
    fpad[cells + 1] = jnp.zeros(fpad.shape[1:], F32)

    def mixed(ref, i, first):
        parts = []
        for c in range(NC):
            high, low = split(ref[i, c].reshape(32, 128))
            parts.append(jnp.concatenate([high, low, high], axis=0))
        return jnp.dot(mix[first], jnp.concatenate(parts, axis=1), preferred_element_type=F32)

    @pl.loop(0, cells)
    def _(i):
        sums = mixed(fpad, i + 1, 0)
        for c in range(NC):
            mine = fpad[i + 1, c]
            flatm = mine.reshape(32, 128)
            around = (fpad[i, c] + fpad[i + 2, c]
                      + (pltpu.roll(flatm, 1, 1) + pltpu.roll(flatm, 127, 1)).reshape(4, 8, 128))
            res[i, c] = (force[i, c] - 1.5 * mine + 0.2 * around
                         + sums[:, 128 * c:128 * c + 128].reshape(4, 8, 128))

    to_mate.wait_recv()

    @pl.when(me > 0)
    def _():
        up.wait_recv()
        res[0] += 0.2 * below[...]

    @pl.when(me < n - 1)
    def _():
        down.wait_recv()
        res[cells - 1] += 0.2 * above[...]

    for c in range(NC):
        swept[0, c] = jnp.zeros((4, 8, 128), F32)
        corr[cells, c] = jnp.zeros((4, 8, 128), F32)

    @pl.loop(0, cells)
    def _(i):
        sums = mixed(other, i, 1)
        rows = []
        for c in range(NC):
            r = res[i, c] + sums[:, 128 * c:128 * c + 128].reshape(4, 8, 128)
            res[i, c] = r
            rows.append(r)
        scaled = apply(from_diag(i), rows)
        new = apply(from_maps(maps, i, 0), [swept[i, c] for c in range(NC)], scaled)
        for a in range(NC):
            swept[i + 1, a] = new[a]

    @pl.loop(0, cells)
    def _(k):
        i = cells - 1 - k
        new = apply(from_maps(maps, i, 2), [corr[i + 1, c] for c in range(NC)],
                    [swept[i + 1, a] for a in range(NC)])
        for a in range(NC):
            corr[i, a] = new[a]

    for a in range(NC):
        summary[32 * a:32 * a + 32] = swept[cells, a].reshape(32, 128)
        summary[160 + 32 * a:192 + 32 * a] = corr[0, a].reshape(32, 128)
    summary[320:384] = jnp.zeros((64, 128), F32)
    scatter_rows(summary[...].T, send_v)
    v_start()
    m_wait()
    bounds[0:256] = gather_rows(got_m).T
    v_wait()
    summary[...] = gather_rows(got_v).T
    lane = lax.broadcasted_iota(jnp.int32, (8, 128), 1)[None]
    steps = n.bit_length() - 1

    def shift(x, by):
        blocks = x.shape[0]
        return pltpu.roll(x.reshape(8 * blocks, 128), by, 1).reshape(blocks, 8, 128)

    for a in range(NC):
        work[0, a, 0:4] = summary[32 * a:32 * a + 32].reshape(4, 8, 128)
        work[0, a, 4:6] = bounds[16 * a:16 * a + 16].reshape(2, 8, 128)
        work[1, a, 4:6] = bounds[160 + 16 * a:176 + 16 * a].reshape(2, 8, 128)

    def scan(which, backward):
        @pl.loop(0, steps)
        def _(k):
            by = jnp.left_shift(per, k)
            turn = 128 - by if backward else by
            inside = lane < 128 - by if backward else lane >= by
            moved = [shift(work[which, c], turn) for c in range(NC)]
            old = [work[which, a] for a in range(NC)]
            start = [jnp.concatenate([old[a][0:4], jnp.zeros((2, 8, 128), F32)], axis=0) for a in range(NC)]
            new = apply(from_maps(work, which, 4), moved, start)
            for a in range(NC):
                work[which, a] = jnp.where(inside, new[a], old[a])

    scan(0, False)
    entering = [jnp.where(lane >= per, shift(work[0, a, 0:4], per), F32(0.0)) for a in range(NC)]

    def from_tail(a, c):
        at = 80 + 16 * a + 2 * c
        return spread(bounds[at:at + 1, :], bounds[at + 1:at + 2, :], mask)

    last = apply(from_tail, entering, [summary[160 + 32 * a:192 + 32 * a].reshape(4, 8, 128) for a in range(NC)])
    for a in range(NC):
        work[1, a, 0:4] = last[a]
        summary[32 * a:32 * a + 32] = entering[a].reshape(32, 128)
    scan(1, True)
    for a in range(NC):
        back = jnp.where(lane < 128 - per, shift(work[1, a, 0:4], 128 - per), F32(0.0))
        summary[160 + 32 * a:192 + 32 * a] = back.reshape(32, 128)
    scatter_rows(summary[...].T, send_r)
    r_start()
    r_wait()
    bounds[...] = gather_rows(got_r).T

    @pl.loop(0, cells)
    def _(i):
        first = [bounds[32 * c:32 * c + 32].reshape(4, 8, 128) for c in range(NC)]
        new = apply(from_maps(tail, i, 0), first, [corr[i, a] for a in range(NC)])
        second = [bounds[160 + 32 * c:192 + 32 * c].reshape(4, 8, 128) for c in range(NC)]
        new = apply(from_maps(tail, i, 2), second, new)
        for a in range(NC):
            correction[i, a] = new[a]

    to_mate.wait_send()

    @pl.when(me < n - 1)
    def _():
        up.wait_send()

    @pl.when(me > 0)
    def _():
        down.wait_send()

    m_sent()
    v_sent()
    r_sent()


def deliver(residual, correction, out_residual, out_correction, sems):
    copies = [pltpu.make_async_copy(src.at[i], dst.at[i], sems.at[k, i])
              for k, (src, dst) in enumerate(((residual, out_residual), (correction, out_correction)))
              for i in range(src.shape[0])]
    for copy in copies:
        copy.start()
    for copy in copies:
        copy.wait()


def pin(x):
    return pltpu.with_memory_space_constraint(x, pltpu.HBM)


def body(n, nps, flow, forcing, op, diag, lower, upper):
    cells = flow.shape[0]
    whole = flow.shape
    state = (cells, NC, 4, 8, 128)
    rows = max(8, 128 // n)
    vmem, dma = pltpu.VMEM, pltpu.SemaphoreType.DMA
    spec_any = pl.BlockSpec(memory_space=pltpu.HBM)
    spec_vmem = pl.BlockSpec(memory_space=pltpu.VMEM)
    residual, correction = pl.pallas_call(
        functools.partial(kernel, n, nps, cells),
        out_shape=[jax.ShapeDtypeStruct(state, F32)] * 2,
        in_specs=[spec_any] * 6,
        out_specs=[spec_vmem, spec_vmem],
        scratch_shapes=[
            vmem((16, 16), F32),
            vmem((cells + 2,) + state[1:], F32),
            vmem(state, F32),
            vmem(state[1:], F32),
            vmem(state[1:], F32),
            vmem(state, F32),
            vmem((3, 50 * cells, 128), F32),
            vmem((3, cells, 56, 128), F32),
            vmem(state, F32),
            vmem((cells + 1, NC, 2, 8, 128), F32),
            vmem((cells + 1,) + state[1:], F32),
            vmem((cells + 1,) + state[1:], F32),
            vmem((cells + 1,) + state[1:], F32),
            vmem((2, 32, 96), BF16),
            vmem((2, NC, 6, 8, 128), F32),
            vmem((384, 128), F32),
            vmem((n, rows, 256), F32),
            vmem((n, rows, 256), F32),
            vmem((n, rows, 384), F32),
            vmem((n, rows, 384), F32),
            vmem((n, rows, 384), F32),
            vmem((n, rows, 384), F32),
            vmem((384, 128), F32),
            dma((6,)), dma((3,)), dma((3,)),
            dma((1,)), dma((1,)), dma((1,)), dma((1,)), dma((1,)), dma((1,)),
        ],
        compiler_params=pltpu.CompilerParams(
            collective_id=0, has_side_effects=True, vmem_limit_bytes=40 * 1024 * 1024),
    )(pin(flow.reshape(state)), pin(forcing.reshape(state)), pin(op),
      pin(diag.reshape(50 * cells, 128)), pin(lower.reshape(50 * cells, 128)), pin(upper.reshape(50 * cells, 128)))
    residual, correction = pl.pallas_call(
        deliver,
        out_shape=[jax.ShapeDtypeStruct(state, F32)] * 2,
        in_specs=[pl.BlockSpec(memory_space=pltpu.VMEM)] * 2,
        out_specs=[spec_any] * 2,
        scratch_shapes=[dma((2, cells))],
        compiler_params=pltpu.CompilerParams(vmem_limit_bytes=8 * 1024 * 1024),
    )(residual, correction)
    return residual.reshape(whole), correction.reshape(whole)


def solution(mesh):
    spec = P("row", None, None, "ps", None)
    return jax.shard_map(
        functools.partial(body, mesh.shape["row"], mesh.shape["ps"]),
        mesh=mesh,
        in_specs=(spec, spec, P(), spec, spec, spec),
        out_specs=(spec, spec),
        check_vma=False,
    )
```
